512 devices in a mesh: grp: 16 (over y, core), blk: 32 (over z, x).
Axes of the slice: x: 4, y: 8, z: 8, core: 2. Of those that a mesh axis runs over, the one named last changes fastest.
Arguments:
- embeddings: float32 [65536, 1024], P(('grp', 'blk'))
- cluster_ids: int32 [65536], P(('grp', 'blk')), may hold values from 0 to 15, as said below
- row_slots: int32 [65536], P(('grp', 'blk')), may hold values from 0 to 15, as said below
- cluster_sizes: int32 [512, 16], P(('grp', 'blk')), may hold values from 0 to 16, as said below
Outputs:
- max_similarity: float32 [65536], P(('grp', 'blk'))
The draws below stay inside these ranges and needn't reach their ends.
Inputs may be any that keep to these rules, and one draw needn't show every extreme that they name: `cluster_ids`: every cluster id is used; every cluster holds many rows. `row_slots`: the rows that one device owns of one cluster have the slots 0 to that count minus 1, each once. `cluster_sizes`: entry [d, c] is the number of rows of cluster c owned by device d (the device at index d of grp+blk); each row of it sums to 128.
All inputs are finite; a program needn't handle non-finite values.
Results may differ from the reference program's by a relative error of at most 0.0003.
Values may be sent and summed in bfloat16 or wider, within the bound.
A program may use at most 64 MiB of HBM per device.

```python
import math
import jax
import jax.numpy as jnp
from jax import lax

D = 1024
ROWS_DEV = 128
CLUSTERS = 16
SEND = 16
DEVICES = 512


topic_count = 8


def cluster_layout(key):
    mean_count = ROWS_DEV // CLUSTERS
    pair_count = CLUSTERS // 2
    key_order, key_bias, key_jitter, key_rows = jax.random.split(key, 4)
    cluster_order = jax.random.permutation(key_order, CLUSTERS)
    cluster_bias = jax.random.randint(key_bias, (pair_count,), -(mean_count // 2), mean_count // 2 + 1)
    jitter = jax.random.randint(key_jitter, (DEVICES, pair_count), -(mean_count // 2), mean_count // 2 + 1)
    imbalance = jnp.clip(cluster_bias[None, :] + jitter, -mean_count, mean_count)
    imbalance = imbalance.at[0, 0].set(mean_count)
    paired = jnp.concatenate([mean_count + imbalance, mean_count - imbalance], axis=1).astype(jnp.int32)
    sizes = jnp.zeros((DEVICES, CLUSTERS), jnp.int32).at[:, cluster_order].set(paired)
    cluster_ends = jnp.cumsum(sizes, axis=1)
    cluster_starts = cluster_ends - sizes
    position = jnp.arange(ROWS_DEV, dtype=jnp.int32)
    sorted_cluster = jnp.sum((position[None, :, None] >= cluster_ends[:, None, :]).astype(jnp.int32), axis=2)
    sorted_slot = position[None, :] - jnp.take_along_axis(cluster_starts, sorted_cluster, axis=1)
    row_keys = jax.random.split(key_rows, DEVICES)
    row_order = jax.vmap(lambda single: jax.random.permutation(single, ROWS_DEV))(row_keys)
    clusters_out = jnp.take_along_axis(sorted_cluster, row_order, axis=1).reshape(-1).astype(jnp.int32)
    slots_out = jnp.take_along_axis(sorted_slot, row_order, axis=1).reshape(-1).astype(jnp.int32)
    return (clusters_out, slots_out, sizes)


def draw_cluster_ids(key, part):
    return cluster_layout(key)[0]


def draw_row_slots(key, part):
    return cluster_layout(key)[1]


def draw_cluster_sizes(key, part):
    return cluster_layout(key)[2]


def draw_embeddings(key, part):
    clusters_of_rows = cluster_layout(key)[0]
    key = jax.random.fold_in(key, 7)
    key_topic = jax.random.fold_in(key, 0)
    key_weight = jax.random.fold_in(key, 1)
    key_noise = jax.random.fold_in(key, 2)
    key_scale = jax.random.fold_in(key, 3)
    key_amplitude = jax.random.fold_in(key, 5)
    rows_total = ROWS_DEV * DEVICES
    topics = jax.random.normal(key_topic, (CLUSTERS, topic_count, D), jnp.float32)
    weights = jax.random.normal(key_weight, (rows_total, topic_count), jnp.float32)
    mixed = jnp.zeros((rows_total, D), jnp.float32)
    for index in range(topic_count):
        mixed = mixed + weights[:, index:index + 1] * topics[:, index, :][clusters_of_rows]
    mixed = mixed / math.sqrt(topic_count)
    noise_part = jax.random.normal(key_noise, (rows_total, D), jnp.float32)
    noise_scale = jnp.exp(jax.random.uniform(key_scale, (rows_total, 1), jnp.float32, math.log(0.5), math.log(2.0)))
    amplitude = jnp.exp(jax.random.uniform(key_amplitude, (rows_total, 1), jnp.float32, 0.0, math.log(10.0)))
    return (amplitude * (mixed + noise_scale * noise_part)).astype(jnp.float32)


def setup_inputs(seed: int = 0) -> dict:
    arg_keys = jax.random.split(jax.random.key(seed), 5)
    embeddings = draw_embeddings(jax.random.fold_in(arg_keys[4], 71), 0)
    cluster_ids = draw_cluster_ids(jax.random.fold_in(arg_keys[4], 71), 0)
    row_slots = draw_row_slots(jax.random.fold_in(arg_keys[4], 71), 0)
    cluster_sizes = draw_cluster_sizes(jax.random.fold_in(arg_keys[4], 71), 0)
    return {"embeddings": embeddings, "cluster_ids": cluster_ids, "row_slots": row_slots, "cluster_sizes": cluster_sizes}


def normalize_rows(embeddings):
    total = lax.optimization_barrier(jnp.sum(embeddings * embeddings, axis=1, keepdims=True))
    return (embeddings * lax.rsqrt(total + 1e-06)).astype(jnp.bfloat16)

def reference(embeddings, cluster_ids, row_slots, cluster_sizes):
    unit_rows = normalize_rows(embeddings)
    rows_total = embeddings.shape[0]
    devices = cluster_sizes.shape[0]
    per_device = rows_total // devices
    owner_dev = jnp.arange(rows_total, dtype=jnp.int32) // per_device
    flat_index = ((cluster_ids * devices + owner_dev) * SEND + row_slots).astype(jnp.int32)
    span_rows = devices * SEND
    buffer = jnp.zeros((CLUSTERS * span_rows, D), jnp.bfloat16).at[flat_index].set(unit_rows)
    buffer = buffer.reshape(CLUSTERS, span_rows, D)
    slot_index = jnp.arange(SEND, dtype=jnp.int32)
    alive_slot = (slot_index[None, None, :] < cluster_sizes.T[:, :, None]).reshape(CLUSTERS, span_rows)
    block_rows = math.gcd(span_rows, 1024)
    column_index = jnp.arange(span_rows, dtype=jnp.int32)

    def per_cluster(cluster_data):
        members, alive_cols = cluster_data

        def per_block(block_id):
            row_block = lax.dynamic_slice_in_dim(members, block_id * block_rows, block_rows, 0)
            scores = jnp.dot(row_block, members.T, preferred_element_type=jnp.float32)
            own_index = block_id * block_rows + jnp.arange(block_rows, dtype=jnp.int32)
            usable = alive_cols[None, :] & (own_index[:, None] != column_index[None, :])
            return lax.optimization_barrier(jnp.max(jnp.where(usable, scores, -4.0), axis=1))
        return lax.map(per_block, jnp.arange(span_rows // block_rows, dtype=jnp.int32)).reshape(span_rows)
    top_score = lax.map(per_cluster, (buffer, alive_slot)).reshape(CLUSTERS * span_rows)
    return top_score[flat_index]
```

```python
import functools

import jax
import jax.numpy as jnp
from jax import lax
from jax.experimental import pallas as pl
from jax.experimental.pallas import tpu as pltpu
from jax.sharding import PartitionSpec as P

MESH = pl.DeviceIdType.MESH
ROWS = 128
WIDTH = 1024
NY, NZ, NX = 8, 8, 4
FLOOR = -4.0

STEPS = ((0, 0, 1), (0, 0, -1), (1, 0, 0), (-1, 0, 0), (0, 1, 0), (0, -1, 0))
EDGES = (
    (0, 2), (0, 5), (0, 4), (3, 4), (1, 0), (0, 3),
    (3, 1), (2, 5), (6, 3), (8, 5), (5, 2), (5, 0),
    (4, 4), (11, 2), (13, 4), (10, 1), (9, 3), (4, 1),
    (14, 0), (7, 1), (9, 0), (17, 3), (14, 2), (16, 5),
)
PARTS = 2
LEFTS, RIGHTS = 2, 4
PHASES = (
    ((2, 4, 6, 12, 3, 5, 7, 13, 10, 14, 8, 16, 18, 11, 15, 22, 9, 17, 19, 24, 36, 23, 20, 26, 34, 40, 42), (3, 5, 6, 2, 0, 11)),
    ((28, 21, 27, 35), (17, 7, 6, 8, 5, 3)),
    ((25, 32), (1, 12, 9, 2, 17, 0)),
    ((), (11, 12, 6, 13, 7, 10)),
    ((29, 30, 44), (14, 9, 4, 6, 3, 10)),
    ((), (17, 14, 7, 2, 13, 10)),
    ((33, 38), (5, 16, 13, 12, 6, 8)),
    ((46, 48, 31, 45), (16, 15, 14, 11, 17, 0)),
    ((), (15, 22, 5, 16, 12, 7)),
    ((37, 39), (18, 8, 9, 1, 12, 14)),
    ((), (11, 18, 22, 3, 15, 1)),
    ((47, 49), (23, 19, 18, 15, 16, 7)),
    ((41, 43), (21, 5, 10, 18, 3, 16)),
    ((), (8, 13, 19, 22, 9, 23)),
    ((), (24, 20, 0, 17, 23, 9)),
    ((), (6, 11, 24, 12, 18, 8)),
    ((), (2, 15, 6, 22, 20, 9)),
    ((), (13, 15, 0, 21, 1, 6)),
    ((), (18, 4, 13, 17, 21, 11)),
    ((), (8, 20, 10, 3, 21, 11)),
)
SLOTS = len(EDGES) + 1
PART = ROWS // PARTS


def tree_offsets():
    offsets = [(0, 0, 0)]
    for parent, way in EDGES:
        offsets.append(tuple(a + b for a, b in zip(offsets[parent], STEPS[way])))
    return offsets


OFFSETS = tree_offsets()
CHILDREN = [[s + 1 for s, edge in enumerate(EDGES) if edge[0] == p] for p in range(SLOTS)]
LEFT_SLOTS = sorted({s for _, batch in PHASES for s in batch[:LEFTS]} | {0})
RIGHT_SLOTS = sorted({s for _, batch in PHASES for s in batch[LEFTS:]} | {0})


def last_use(slot):
    return max((k for k, (_, batch) in enumerate(PHASES) if slot in batch), default=0)


def first_right(slot):
    return min((k for k, (_, batch) in enumerate(PHASES) if slot in batch[LEFTS:]), default=0)


def normalize_rows(block):
    total = jnp.sum(block * block, axis=1, keepdims=True)
    return (block * lax.rsqrt(total + 1e-06)).astype(jnp.bfloat16)


def column_ids(row):
    return jnp.transpose(jnp.broadcast_to(row, (ROWS, ROWS)))


def kernel(
    rows_ref, ids_ref, out_ref,
    mine, other, ids, row_best, col_best, own_out, own_in, cross_out, cross_in,
    part_send, part_recv, ids_send, ids_recv, pair_send, pair_recv,
    own_send, own_recv, cross_send, cross_recv,
):
    grp = lax.axis_index("grp")
    blk = lax.axis_index("blk")
    y, core, z, x = grp // 2, grp % 2, blk // NX, blk % NX

    def at(offset, flip=False):
        ty = (y + offset[0] + 4 * NY) % NY
        tz = (z + offset[1] + 4 * NZ) % NZ
        tx = (x + offset[2] + 4 * NX) % NX
        return (ty * 2 + (1 - core if flip else core), tz * NX + tx)

    def negated(offset):
        return tuple(-a for a in offset)

    sibling = at((0, 0, 0), True)

    def part(slot, c):
        return pl.ds(slot * ROWS + c * PART, PART)

    def edge_copy(slot, c):
        parent, way = EDGES[slot - 1]
        return pltpu.make_async_remote_copy(
            src_ref=mine.at[part(parent, c)], dst_ref=mine.at[part(slot, c)],
            send_sem=part_send.at[slot, c], recv_sem=part_recv.at[slot, c],
            device_id=at(negated(STEPS[way])), device_id_type=MESH)

    def ids_copy(slot):
        if slot == 0:
            return pltpu.make_async_remote_copy(
                src_ref=ids.at[0, 0], dst_ref=ids.at[0, 1],
                send_sem=ids_send.at[0], recv_sem=ids_recv.at[0],
                device_id=sibling, device_id_type=MESH)
        parent, way = EDGES[slot - 1]
        return pltpu.make_async_remote_copy(
            src_ref=ids.at[parent], dst_ref=ids.at[slot],
            send_sem=ids_send.at[slot], recv_sem=ids_recv.at[slot],
            device_id=at(negated(STEPS[way])), device_id_type=MESH)

    def pair_copy(slot):
        return pltpu.make_async_remote_copy(
            src_ref=mine.at[pl.ds(slot * ROWS, ROWS)], dst_ref=other.at[pl.ds(slot * ROWS, ROWS)],
            send_sem=pair_send.at[slot], recv_sem=pair_recv.at[slot],
            device_id=sibling, device_id_type=MESH)

    def own_copy(slot):
        return pltpu.make_async_remote_copy(
            src_ref=own_out.at[slot], dst_ref=own_in.at[slot],
            send_sem=own_send.at[slot], recv_sem=own_recv.at[slot],
            device_id=at(OFFSETS[slot]), device_id_type=MESH)

    def cross_copy(slot):
        return pltpu.make_async_remote_copy(
            src_ref=cross_out.at[slot], dst_ref=cross_in.at[slot],
            send_sem=cross_send.at[slot], recv_sem=cross_recv.at[slot],
            device_id=at(OFFSETS[slot], True), device_id_type=MESH)

    barrier = pltpu.get_barrier_semaphore()
    peers = [at(step) for step in STEPS] + [sibling]
    for peer in peers:
        pl.semaphore_signal(barrier, inc=1, device_id=peer, device_id_type=MESH)

    ids[0, 0] = ids_ref[...]
    mine[0:PART, :] = normalize_rows(rows_ref[0:PART, :])
    pl.semaphore_wait(barrier, len(peers))
    for c in range(PARTS):
        if c > 0:
            mine[c * PART:(c + 1) * PART, :] = normalize_rows(rows_ref[c * PART:(c + 1) * PART, :])
        for child in CHILDREN[0]:
            edge_copy(child, c).start()
        if c == 0:
            ids_copy(0).start()
    pair_copy(0).start()
    row_best[...] = jnp.full_like(row_best, FLOOR)
    col_best[...] = jnp.full_like(col_best, FLOOR)
    ids_copy(0).wait()
    for child in CHILDREN[0]:
        ids_copy(child).start()

    def arrive(slot, c):
        edge_copy(slot, c).wait_recv()
        for child in CHILDREN[slot]:
            edge_copy(child, c).start()
        if c == 0:
            ids_copy(slot).wait_recv()
            for child in CHILDREN[slot]:
                ids_copy(child).start()
        if c == PARTS - 1 and slot in RIGHT_SLOTS:
            pair_copy(slot).start()

    def finish(slot):
        if slot in RIGHT_SLOTS:
            columns = jnp.max(col_best[slot], axis=0, keepdims=True)
            cross_out[slot] = columns[:, ROWS:]
            cross_copy(slot).start()
        if slot in LEFT_SLOTS:
            best = jnp.max(jnp.transpose(row_best[pl.ds(slot * ROWS, ROWS), :]), axis=0, keepdims=True)
            if slot in RIGHT_SLOTS:
                best = jnp.maximum(best, columns[:, :ROWS])
        else:
            best = columns[:, :ROWS]
        own_out[slot] = best
        if slot > 0:
            own_copy(slot).start()

    def own_block():
        left = mine[0:ROWS, :]
        right = jnp.concatenate([left, other[0:ROWS, :]], axis=0)
        scores = lax.dot_general(
            left, right, (((1,), (1,)), ((), ())), preferred_element_type=jnp.float32)
        down = column_ids(ids[0, 0])
        same = lax.broadcasted_iota(jnp.int32, (ROWS, ROWS), 0) == lax.broadcasted_iota(
            jnp.int32, (ROWS, ROWS), 1)
        near = jnp.where((down == ids[0, 0]) & jnp.logical_not(same), scores[:, :ROWS], FLOOR)
        far = jnp.where(down == ids[0, 1], scores[:, ROWS:], FLOOR)
        row_best[0:ROWS, :] = jnp.maximum(near, far)

    def events(phase):
        for arrival in PHASES[phase][0]:
            arrive(arrival // PARTS, arrival % PARTS)
        for slot in RIGHT_SLOTS:
            if slot > 0 and first_right(slot) == phase:
                pair_copy(slot).wait_recv()

    def batch(phase):
        code = jnp.int32(0)
        for k, (_, slots) in enumerate(PHASES):
            code = jnp.where(phase == k, sum(s << (5 * i) for i, s in enumerate(slots)), code)
        picked = [(code >> (5 * i)) & 31 for i in range(LEFTS + RIGHTS)]
        lefts, rights = picked[:LEFTS], picked[LEFTS:]

        def span(slot):
            return pl.ds(pl.multiple_of(slot * ROWS, ROWS), ROWS)

        left = jnp.concatenate([mine[span(s), :] for s in lefts], axis=0)
        right = jnp.concatenate([m[span(s), :] for s in rights for m in (mine, other)], axis=0)
        scores = lax.dot_general(
            left, right, (((1,), (1,)), ((), ())), preferred_element_type=jnp.float32)
        for i, a in enumerate(lefts):
            down = column_ids(ids[a, 0])
            best = row_best[span(a), :]
            for j, b in enumerate(rights):
                for half in range(2):
                    lane = (2 * j + half) * ROWS
                    block = scores[i * ROWS:(i + 1) * ROWS, lane:lane + ROWS]
                    block = jnp.where(down == ids[b, half], block, FLOOR)
                    best = jnp.maximum(best, block)
                    top = jnp.max(block.reshape(ROWS // 8, 8, ROWS), axis=0)
                    span_half = slice(half * ROWS, (half + 1) * ROWS)
                    col_best[b, :, span_half] = jnp.maximum(col_best[b, :, span_half], top)
            row_best[span(a), :] = best

    pair_copy(0).wait_recv()
    own_block()

    def step(phase, carry):
        for k in range(len(PHASES)):
            pl.when(phase == k)(functools.partial(events, k))
        batch(phase)
        for k in range(len(PHASES)):
            done = [s for s in range(SLOTS) if last_use(s) == k]
            if done:
                def close(done=done):
                    for slot in done:
                        finish(slot)
                pl.when(phase == k)(close)
        return carry

    lax.fori_loop(0, len(PHASES), step, 0)

    for slot in range(1, SLOTS):
        for c in range(PARTS):
            edge_copy(slot, c).wait_send()
        ids_copy(slot).wait_send()
    for slot in RIGHT_SLOTS:
        pair_copy(slot).wait_send()
    for slot in range(SLOTS):
        if slot > 0:
            own_copy(slot).wait_send()
        if slot in RIGHT_SLOTS:
            cross_copy(slot).wait_send()
    best = own_out[0]
    for slot in range(SLOTS):
        if slot > 0:
            own_copy(slot).wait_recv()
            best = jnp.maximum(best, own_in[slot])
        if slot in RIGHT_SLOTS:
            cross_copy(slot).wait_recv()
            best = jnp.maximum(best, cross_in[slot])
    out_ref[...] = best


def body(embeddings, cluster_ids, row_slots, cluster_sizes):
    dma = pltpu.SemaphoreType.DMA
    best = pl.pallas_call(
        kernel,
        out_shape=jax.ShapeDtypeStruct((1, ROWS), jnp.float32),
        in_specs=[pl.BlockSpec(memory_space=pltpu.VMEM)] * 2,
        out_specs=pl.BlockSpec(memory_space=pltpu.VMEM),
        scratch_shapes=[
            pltpu.VMEM((SLOTS * ROWS, WIDTH), jnp.bfloat16),
            pltpu.VMEM((SLOTS * ROWS, WIDTH), jnp.bfloat16),
            pltpu.VMEM((SLOTS, 2, 1, ROWS), jnp.int32),
            pltpu.VMEM((SLOTS * ROWS, ROWS), jnp.float32),
            pltpu.VMEM((SLOTS, 8, 2 * ROWS), jnp.float32),
            pltpu.VMEM((SLOTS, 1, ROWS), jnp.float32),
            pltpu.VMEM((SLOTS, 1, ROWS), jnp.float32),
            pltpu.VMEM((SLOTS, 1, ROWS), jnp.float32),
            pltpu.VMEM((SLOTS, 1, ROWS), jnp.float32),
            dma((SLOTS, PARTS)), dma((SLOTS, PARTS)), dma((SLOTS,)), dma((SLOTS,)),
            dma((SLOTS,)), dma((SLOTS,)), dma((SLOTS,)), dma((SLOTS,)),
            dma((SLOTS,)), dma((SLOTS,)),
        ],
        compiler_params=pltpu.CompilerParams(
            collective_id=1, has_side_effects=True, vmem_limit_bytes=48 * 2**20),
    )(embeddings, cluster_ids.reshape(1, ROWS))
    return best.reshape(ROWS)


def solution(mesh):
    placed = (
        P(("grp", "blk"), None),
        P(("grp", "blk")),
        P(("grp", "blk")),
        P(("grp", "blk"), None),
    )
    return jax.shard_map(
        body, mesh=mesh, in_specs=placed, out_specs=P(("grp", "blk")), check_vma=False
    )
```

```python
import functools

import jax
import jax.numpy as jnp
from jax import lax
from jax.experimental import pallas as pl
from jax.experimental.pallas import tpu as pltpu
from jax.sharding import PartitionSpec as P

MESH = pl.DeviceIdType.MESH
ROWS = 128
WIDTH = 1024
NY, NZ, NX = 8, 8, 4
FLOOR = -4.0

STEPS = ((0, 0, 1), (0, 0, -1), (1, 0, 0), (-1, 0, 0), (0, 1, 0), (0, -1, 0))
EDGES = (
    (0, 3), (1, 1), (0, 2), (0, 5), (4, 0), (5, 5),
    (0, 4), (7, 4), (6, 5), (3, 2), (10, 2), (1, 3),
    (11, 0), (12, 1), (2, 1), (14, 3), (9, 5), (8, 4),
    (16, 3), (9, 0), (7, 0), (20, 4), (11, 2), (17, 1),
)
PARTS = 4
FIRST = (15, 5, 35, 20, 16, 6, 36, 21, 17, 7, 37, 22)
PHASES = (
    ((10, 105, 25, 18, 8, 38, 23, 11, 26, 50, 60, 40, 75, 12, 27, 51, 61, 41, 30, 19, 9, 24, 39, 13, 28, 52, 62, 42, 31, 70, 106), (1, 0)),
    ((53, 63, 43), (3, 1)),
    ((32,), (4, 0, 1, 3)),
    ((107, 71, 55, 90, 45), (7, 4)),
    ((14, 29, 33, 72, 108, 56, 91, 80, 54, 64), (2, 1, 3, 4, 7)),
    ((73, 57, 92, 46, 44), (5, 0, 2, 3, 7)),
    ((100, 81, 47, 76, 65, 58, 93, 95, 34, 109, 82, 48, 77, 66, 115, 74, 110), (6, 1, 2, 3, 7)),
    ((101, 78, 116, 83, 85), (8, 1, 2, 3, 4, 6)),
    ((), (10, 2, 5, 6, 7, 8)),
    ((102, 117, 96, 86, 59, 94), (12, 7, 10, 2, 5, 6, 8)),
    ((49,), (14, 10, 5, 6, 7, 8)),
    ((103, 118, 97, 87), (21, 3, 2, 4, 0, 10, 14)),
    ((120, 84, 79, 111, 98), (9, 1, 2, 3, 10, 12, 14, 21)),
    ((67, 88), (11, 4, 5, 6, 7, 8, 9, 14, 21)),
    ((68, 121, 112), (16, 7, 5, 6, 8, 9, 11, 21)),
    ((122,), (18, 1, 2, 3, 10, 11, 12, 14, 16)),
    ((113, 104, 119), (15, 11, 10, 0, 1, 3, 6, 8, 18)),
    ((123, 89, 99), (20, 2, 0, 7, 10, 11, 14, 16)),
    ((69, 114), (17, 3, 10, 11, 12, 14, 16)),
    ((), (19, 4, 5, 6, 7, 8, 9, 17, 18)),
    ((124,), (22, 4, 10, 11, 14, 16)),
    ((), (23, 1, 7, 6, 8, 9, 17, 18)),
    ((), (13, 10, 6, 7, 8, 9, 17, 18)),
    ((), (24, 5, 2, 15, 22, 1, 10, 13, 23)),
)
SLOTS = len(EDGES) + 1
PART = ROWS // PARTS


def tree_offsets():
    offsets = [(0, 0, 0)]
    for parent, way in EDGES:
        offsets.append(tuple(a + b for a, b in zip(offsets[parent], STEPS[way])))
    return offsets


OFFSETS = tree_offsets()
CHILDREN = [[s + 1 for s, edge in enumerate(EDGES) if edge[0] == p] for p in range(SLOTS)]
ORDER = [slots[0] for _, slots in PHASES]
SIZES = (4, 6, 8)


def last_use(slot):
    return max((k for k, (_, slots) in enumerate(PHASES) if slot in slots), default=0)


def size_of(slots):
    return min(size for size in SIZES if size >= len(slots) - 1)


def padded(slots):
    return slots + slots[-1:] * (SIZES[-1] + 1 - len(slots))


def normalize_rows(block):
    total = jnp.sum(block * block, axis=1, keepdims=True)
    return (block * lax.rsqrt(total + 1e-06)).astype(jnp.bfloat16)


def column_ids(row):
    return jnp.transpose(jnp.broadcast_to(row, (ROWS, ROWS)))


def kernel(
    rows_hbm, ids_hbm, out_ref,
    rows_ref, mine, other, ids, down_ids, row_best, col_best, own_out, own_in, cross_out, cross_in,
    part_send, part_recv, ids_send, ids_recv, pair_send, pair_recv,
    own_send, own_recv, cross_send, cross_recv, load_sem,
):
    grp = lax.axis_index("grp")
    blk = lax.axis_index("blk")
    y, core, z, x = grp // 2, grp % 2, blk // NX, blk % NX

    def at(offset, flip=False):
        ty = lax.rem(y + offset[0] % NY, NY)
        tz = lax.rem(z + offset[1] % NZ, NZ)
        tx = lax.rem(x + offset[2] % NX, NX)
        return (ty * 2 + (1 - core if flip else core), tz * NX + tx)

    def negated(offset):
        return tuple(-a for a in offset)

    sibling = at((0, 0, 0), True)
    behind = [at(negated(step)) for step in STEPS]

    def part(slot, c):
        return pl.ds(slot * ROWS + c * PART, PART)

    def edge_copy(slot, c):
        parent, way = EDGES[slot - 1]
        return pltpu.make_async_remote_copy(
            src_ref=mine.at[part(parent, c)], dst_ref=mine.at[part(slot, c)],
            send_sem=part_send.at[0], recv_sem=part_recv.at[slot, c],
            device_id=behind[way], device_id_type=MESH)

    def ids_copy(slot):
        if slot == 0:
            return pltpu.make_async_remote_copy(
                src_ref=ids.at[0, 0], dst_ref=ids.at[0, 1],
                send_sem=ids_send.at[0], recv_sem=ids_recv.at[0],
                device_id=sibling, device_id_type=MESH)
        parent, way = EDGES[slot - 1]
        return pltpu.make_async_remote_copy(
            src_ref=ids.at[parent], dst_ref=ids.at[slot],
            send_sem=ids_send.at[1], recv_sem=ids_recv.at[slot],
            device_id=behind[way], device_id_type=MESH)

    def pair_copy(slot):
        return pltpu.make_async_remote_copy(
            src_ref=mine.at[pl.ds(slot * ROWS, ROWS)], dst_ref=other.at[pl.ds(slot * ROWS, ROWS)],
            send_sem=pair_send.at[0], recv_sem=pair_recv.at[slot],
            device_id=sibling, device_id_type=MESH)

    def own_copy(slot):
        return pltpu.make_async_remote_copy(
            src_ref=own_out.at[slot], dst_ref=own_in.at[slot],
            send_sem=own_send.at[0], recv_sem=own_recv.at[0],
            device_id=at(OFFSETS[slot]), device_id_type=MESH)

    def cross_copy(slot):
        return pltpu.make_async_remote_copy(
            src_ref=cross_out.at[slot], dst_ref=cross_in.at[slot],
            send_sem=cross_send.at[0], recv_sem=cross_recv.at[0],
            device_id=at(OFFSETS[slot], True), device_id_type=MESH)

    barrier = pltpu.get_barrier_semaphore()
    peers = behind + [sibling]
    for peer in peers:
        pl.semaphore_signal(barrier, inc=1, device_id=peer, device_id_type=MESH)

    loads = [
        pltpu.make_async_copy(
            rows_hbm.at[pl.ds(c * PART, PART)], rows_ref.at[pl.ds(c * PART, PART)], load_sem.at[c])
        for c in range(PARTS)]
    loads.append(pltpu.make_async_copy(ids_hbm, ids.at[0, 0], load_sem.at[PARTS]))
    for load in loads:
        load.start()

    def normalize_part(c):
        loads[c].wait()
        mine[c * PART:(c + 1) * PART, :] = normalize_rows(rows_ref[c * PART:(c + 1) * PART, :])

    normalize_part(0)
    loads[PARTS].wait()
    pl.semaphore_wait(barrier, len(peers))
    ids_copy(0).start()
    taken = set()

    def take(slot, c):
        if slot > 0 and (slot, c) not in taken:
            taken.add((slot, c))
            edge_copy(slot, c).wait_recv()

    def take_ids(slot):
        if (slot, PARTS) not in taken:
            taken.add((slot, PARTS))
            if slot == 0:
                ids_copy(0).wait()
            else:
                ids_copy(slot).wait_recv()

    def take_block(slot):
        for c in range(PARTS):
            take(slot, c)
        take_ids(slot)

    def take_pair(slot):
        if (slot, PARTS + 1) not in taken:
            taken.add((slot, PARTS + 1))
            pair_copy(slot).wait_recv()

    def act(action):
        slot, c = action // (PARTS + 1), action % (PARTS + 1)
        if c == PARTS:
            for part_ in range(PARTS):
                take(slot, part_)
            pair_copy(slot).start()
            return
        parent = EDGES[slot - 1][0]
        take(parent, c)
        if c == PARTS - 1:
            take_ids(parent)
            ids_copy(slot).start()
        edge_copy(slot, c).start()

    def finish(slot):
        best = jnp.max(jnp.transpose(row_best[span(slot), :]), axis=0, keepdims=True)
        if slot > 0:
            best = jnp.maximum(best, col_best[slot])
        own_out[slot] = best
        if slot > 0:
            own_copy(slot).start()

    def span(slot):
        if isinstance(slot, int):
            return pl.ds(slot * ROWS, ROWS)
        return pl.ds(pl.multiple_of(slot * ROWS, ROWS), ROWS)

    def own_block():
        left = mine[0:ROWS, :]
        right = jnp.concatenate([left, other[0:ROWS, :]], axis=0)
        scores = lax.dot_general(
            left, right, (((1,), (1,)), ((), ())), preferred_element_type=jnp.float32)
        down = column_ids(ids[0, 0])
        down_ids[0:ROWS, :] = down
        same = lax.broadcasted_iota(jnp.int32, (ROWS, ROWS), 0) == lax.broadcasted_iota(
            jnp.int32, (ROWS, ROWS), 1)
        near = jnp.where((down == ids[0, 0]) & jnp.logical_not(same), scores[:, :ROWS], FLOOR)
        far = jnp.where(down == ids[0, 1], scores[:, ROWS:], FLOOR)
        row_best[0:ROWS, :] = jnp.maximum(near, far)

    def events(phase):
        if phase > 0:
            cross_copy(ORDER[phase - 1]).start()
            for slot in range(SLOTS):
                if last_use(slot) == phase - 1:
                    finish(slot)
        if phase < len(PHASES):
            actions, slots = PHASES[phase]
            for action in actions:
                act(action)
            take_block(slots[0])
            take_pair(slots[0])

    def lookup(phase, values):
        found = jnp.int32(values[0])
        for k, value in enumerate(values[1:], 1):
            found = jnp.where(phase == k, value, found)
        return found

    def packed(phase, first, count):
        code = lookup(phase, [
            sum(s << (5 * i) for i, s in enumerate(padded(slots)[first:first + count]))
            for _, slots in PHASES])
        return [(code >> (5 * i)) & 31 for i in range(count)]

    def products(new, partners):
        left = jnp.concatenate([mine[span(p), :] for p in partners], axis=0)
        right = jnp.concatenate([mine[span(new), :], other[span(new), :]], axis=0)
        scores = lax.dot_general(
            left, right, (((1,), (1,)), ((), ())), preferred_element_type=jnp.float32)
        down_ids[span(new), :] = column_ids(ids[new, 0])
        top = [jnp.full((8, ROWS), FLOOR, jnp.float32)] * 2
        for i, p in enumerate(partners):
            down = down_ids[span(p), :]
            best = row_best[span(p), :]
            for half in range(2):
                block = scores[i * ROWS:(i + 1) * ROWS, half * ROWS:(half + 1) * ROWS]
                block = jnp.where(down == ids[new, half], block, FLOOR)
                best = jnp.maximum(best, block)
                top[half] = jnp.maximum(
                    top[half], jnp.max(block.reshape(ROWS // 8, 8, ROWS), axis=0))
            row_best[span(p), :] = best
        col_best[new] = jnp.max(top[0], axis=0, keepdims=True)
        cross_out[new] = jnp.max(top[1], axis=0, keepdims=True)

    def batch(phase):
        new, *partners = packed(phase, 0, 5) + packed(phase, 5, 4)
        size = lookup(phase, [size_of(slots) for _, slots in PHASES])
        for count in SIZES:
            if any(size_of(slots) == count for _, slots in PHASES):
                pl.when(size == count)(lambda count=count: products(new, partners[:count]))

    def dispatch(phase, low, high):
        if high - low == 1:
            events(low)
            return
        middle = (low + high) // 2
        pl.when(phase < middle)(lambda: dispatch(phase, low, middle))
        pl.when(phase >= middle)(lambda: dispatch(phase, middle, high))

    for c in range(PARTS):
        if c > 0:
            normalize_part(c)
        for action in FIRST:
            if action % (PARTS + 1) == c:
                act(action)
    act(PARTS)
    row_best[...] = jnp.full_like(row_best, FLOOR)
    take_pair(0)
    take_ids(0)
    own_block()

    def step(phase, carry):
        dispatch(phase, 0, len(PHASES))
        batch(phase)
        return carry

    lax.fori_loop(0, len(PHASES), step, 0)
    events(len(PHASES))

    def whole(ref, send, recv, first, count):
        rows = ref.at[pl.ds(first, count)]
        return pltpu.make_async_remote_copy(
            src_ref=rows, dst_ref=rows, send_sem=send.at[0], recv_sem=recv.at[0],
            device_id=sibling, device_id_type=MESH)

    whole(mine, part_send, part_send, 0, (SLOTS - 1) * ROWS).wait_send()
    whole(mine, pair_send, pair_send, 0, SLOTS * ROWS).wait_send()
    whole(ids, ids_send.at[pl.ds(1, 1)], ids_send.at[pl.ds(1, 1)], 0, SLOTS - 1).wait_send()
    own = whole(own_in, own_send, own_recv, 1, SLOTS - 1)
    cross = whole(cross_in, cross_send, cross_recv, 1, SLOTS - 1)
    own.wait_send()
    cross.wait_send()
    cross.wait_recv()
    own.wait_recv()
    best = own_out[0]
    for slot in range(1, SLOTS):
        best = jnp.maximum(best, jnp.maximum(own_in[slot], cross_in[slot]))
    out_ref[...] = best


def body(embeddings, cluster_ids, row_slots, cluster_sizes):
    dma = pltpu.SemaphoreType.DMA
    best = pl.pallas_call(
        kernel,
        out_shape=jax.ShapeDtypeStruct((1, ROWS), jnp.float32),
        in_specs=[pl.BlockSpec(memory_space=pl.ANY)] * 2,
        out_specs=pl.BlockSpec(memory_space=pltpu.VMEM),
        scratch_shapes=[
            pltpu.VMEM((ROWS, WIDTH), jnp.float32),
            pltpu.VMEM((SLOTS * ROWS, WIDTH), jnp.bfloat16),
            pltpu.VMEM((SLOTS * ROWS, WIDTH), jnp.bfloat16),
            pltpu.VMEM((SLOTS, 2, 1, ROWS), jnp.int32),
            pltpu.VMEM((SLOTS * ROWS, ROWS), jnp.int32),
            pltpu.VMEM((SLOTS * ROWS, ROWS), jnp.float32),
            pltpu.VMEM((SLOTS, 1, ROWS), jnp.float32),
            pltpu.VMEM((SLOTS, 1, ROWS), jnp.float32),
            pltpu.VMEM((SLOTS, 1, ROWS), jnp.float32),
            pltpu.VMEM((SLOTS, 1, ROWS), jnp.float32),
            pltpu.VMEM((SLOTS, 1, ROWS), jnp.float32),
            dma((1,)), dma((SLOTS, PARTS)), dma((2,)), dma((SLOTS,)),
            dma((1,)), dma((SLOTS,)), dma((1,)), dma((1,)),
            dma((1,)), dma((1,)), dma((PARTS + 1,)),
        ],
        compiler_params=pltpu.CompilerParams(
            collective_id=1, has_side_effects=True, vmem_limit_bytes=63 * 2**20),
    )(embeddings, cluster_ids.reshape(1, ROWS))
    return best.reshape(ROWS)


def solution(mesh):
    placed = (
        P(("grp", "blk"), None),
        P(("grp", "blk")),
        P(("grp", "blk")),
        P(("grp", "blk"), None),
    )
    return jax.shard_map(
        body, mesh=mesh, in_specs=placed, out_specs=P(("grp", "blk")), check_vma=False
    )
```

```python
import functools

import jax
import jax.numpy as jnp
from jax import lax
from jax.experimental import pallas as pl
from jax.experimental.pallas import tpu as pltpu
from jax.sharding import PartitionSpec as P

MESH = pl.DeviceIdType.MESH
ROWS = 128
WIDTH = 1024
NY, NZ, NX = 8, 8, 4
FLOOR = -4.0

STEPS = ((0, 0, 1), (0, 0, -1), (1, 0, 0), (-1, 0, 0), (0, 1, 0), (0, -1, 0))
EDGES = (
    (0, 3), (1, 3), (2, 3), (3, 0), (0, 1), (0, 2),
    (6, 2), (3, 3), (5, 5), (0, 4), (10, 4), (9, 5),
    (6, 0), (11, 4), (13, 0), (11, 1), (12, 5), (7, 2),
    (17, 1), (13, 2), (14, 4), (8, 0), (9, 1), (17, 5),
)
PARTS = 4
FIRST = (25, 30, 5, 50, 26, 31, 6, 51, 27, 32, 7, 52, 28, 33, 8, 53)
PHASES = (
    ((45, 65, 35, 10, 55, 46, 66, 36, 11, 56, 47, 67, 115, 60, 75, 37, 12, 57, 29, 34, 9, 54, 48, 68, 116, 38, 13, 58, 80, 61, 76), (1, 0)),
    ((117,), (5, 0)),
    ((90, 15, 70), (6, 1, 5)),
    ((77, 81, 62), (10, 1, 6)),
    ((91, 16, 71, 85, 49, 69, 78, 118, 92, 17, 72, 39, 14, 59, 63, 82), (9, 1, 6)),
    ((93, 18, 73, 20, 86), (2, 6, 5, 9, 10)),
    ((83,), (11, 5, 0, 1, 2, 6)),
    ((21, 100, 40, 105, 87, 79, 95, 119, 101, 41, 106, 22, 120, 64), (23, 6, 11, 10, 2)),
    ((), (13, 10, 23)),
    ((23, 96, 102, 42, 107, 88, 19, 74, 94), (12, 9, 1, 2, 6, 11, 13), (7, 2, 5, 9, 10, 11, 12, 23)),
    ((110, 97, 103, 43, 108, 121, 84), (3, 2, 5, 13, 9, 10, 11, 12)),
    ((111,), (14, 5, 1, 2, 3, 6, 7, 13, 23), (15, 2, 0, 3, 6, 10, 11, 12, 14)),
    ((112, 122, 98, 24, 89), (16, 11, 3, 6, 9, 2, 10, 12), (18, 15, 9, 10, 11, 12, 14, 16, 23)),
    ((113, 123, 44, 104, 109), (17, 14, 1, 2, 3, 6, 7, 15, 18), (4, 7, 9, 10, 12, 14, 16, 17, 23)),
    ((99,), (8, 9, 10, 11, 12, 14, 16, 17, 23), (20, 15, 11, 17, 10, 12, 14, 16, 23)),
    ((114, 124), (21, 6, 2, 3, 4, 8, 13, 15, 20), (19, 12, 6, 2, 4, 8, 18, 20, 21)),
    ((), (24, 23, 15, 2, 4, 18, 20), (22, 23, 16, 19, 21, 24)),
)
SLOTS = len(EDGES) + 1
PART = ROWS // PARTS


def tree_offsets():
    offsets = [(0, 0, 0)]
    for parent, way in EDGES:
        offsets.append(tuple(a + b for a, b in zip(offsets[parent], STEPS[way])))
    return offsets


OFFSETS = tree_offsets()
CHILDREN = [[s + 1 for s, edge in enumerate(EDGES) if edge[0] == p] for p in range(SLOTS)]
SINGLE, DOUBLE = (4, 6, 8), (6, 8)
WIDEST = 8


def last_use(slot):
    return max((k for k, (_, *groups) in enumerate(PHASES) if any(slot in g for g in groups)), default=0)


def shape_of(groups):
    sizes = SINGLE if len(groups) == 1 else DOUBLE
    return len(groups), min(s for s in sizes if s >= max(len(g) for g in groups) - 1)


SHAPES = sorted({shape_of(groups) for _, *groups in PHASES})


def padded(group):
    return group + group[-1:] * (WIDEST + 1 - len(group))


def normalize_rows(block):
    total = jnp.sum(block * block, axis=1, keepdims=True)
    return (block * lax.rsqrt(total + 1e-06)).astype(jnp.bfloat16)


def column_ids(row):
    return jnp.transpose(jnp.broadcast_to(row, (ROWS, ROWS)))


def kernel(
    rows_hbm, ids_hbm, out_ref,
    rows_ref, mine, other, ids, down_ids, row_best, col_best, own_out, own_in, cross_out, cross_in,
    part_send, part_recv, ids_send, ids_recv, pair_send, pair_recv,
    own_send, own_recv, cross_send, cross_recv, load_sem,
):
    grp = lax.axis_index("grp")
    blk = lax.axis_index("blk")
    y, core, z, x = grp // 2, grp % 2, blk // NX, blk % NX

    def at(offset, flip=False):
        ty = lax.rem(y + offset[0] % NY, NY)
        tz = lax.rem(z + offset[1] % NZ, NZ)
        tx = lax.rem(x + offset[2] % NX, NX)
        return (ty * 2 + (1 - core if flip else core), tz * NX + tx)

    def negated(offset):
        return tuple(-a for a in offset)

    sibling = at((0, 0, 0), True)
    behind = [at(negated(step)) for step in STEPS]

    def part(slot, c):
        return pl.ds(slot * ROWS + c * PART, PART)

    def edge_copy(slot, c):
        parent, way = EDGES[slot - 1]
        return pltpu.make_async_remote_copy(
            src_ref=mine.at[part(parent, c)], dst_ref=mine.at[part(slot, c)],
            send_sem=part_send.at[0], recv_sem=part_recv.at[slot, c],
            device_id=behind[way], device_id_type=MESH)

    def ids_copy(slot):
        if slot == 0:
            return pltpu.make_async_remote_copy(
                src_ref=ids.at[0, 0], dst_ref=ids.at[0, 1],
                send_sem=ids_send.at[0], recv_sem=ids_recv.at[0],
                device_id=sibling, device_id_type=MESH)
        parent, way = EDGES[slot - 1]
        return pltpu.make_async_remote_copy(
            src_ref=ids.at[parent], dst_ref=ids.at[slot],
            send_sem=ids_send.at[1], recv_sem=ids_recv.at[slot],
            device_id=behind[way], device_id_type=MESH)

    def pair_copy(slot):
        return pltpu.make_async_remote_copy(
            src_ref=mine.at[pl.ds(slot * ROWS, ROWS)], dst_ref=other.at[pl.ds(slot * ROWS, ROWS)],
            send_sem=pair_send.at[0], recv_sem=pair_recv.at[slot],
            device_id=sibling, device_id_type=MESH)

    def own_copy(slot):
        return pltpu.make_async_remote_copy(
            src_ref=own_out.at[slot], dst_ref=own_in.at[slot],
            send_sem=own_send.at[0], recv_sem=own_recv.at[0],
            device_id=at(OFFSETS[slot]), device_id_type=MESH)

    def cross_copy(slot):
        return pltpu.make_async_remote_copy(
            src_ref=cross_out.at[slot], dst_ref=cross_in.at[slot],
            send_sem=cross_send.at[0], recv_sem=cross_recv.at[0],
            device_id=at(OFFSETS[slot], True), device_id_type=MESH)

    barrier = pltpu.get_barrier_semaphore()
    peers = behind + [sibling]
    for peer in peers:
        pl.semaphore_signal(barrier, inc=1, device_id=peer, device_id_type=MESH)

    loads = [
        pltpu.make_async_copy(
            rows_hbm.at[pl.ds(c * PART, PART)], rows_ref.at[pl.ds(c * PART, PART)], load_sem.at[c])
        for c in range(PARTS)]
    loads.append(pltpu.make_async_copy(ids_hbm, ids.at[0, 0], load_sem.at[PARTS]))
    for load in loads:
        load.start()

    def normalize_part(c):
        loads[c].wait()
        mine[c * PART:(c + 1) * PART, :] = normalize_rows(rows_ref[c * PART:(c + 1) * PART, :])

    normalize_part(0)
    loads[PARTS].wait()
    pl.semaphore_wait(barrier, len(peers))
    ids_copy(0).start()
    taken = set()

    def take(slot, c):
        if slot > 0 and (slot, c) not in taken:
            taken.add((slot, c))
            edge_copy(slot, c).wait_recv()

    def take_ids(slot):
        if (slot, PARTS) not in taken:
            taken.add((slot, PARTS))
            if slot == 0:
                ids_copy(0).wait()
            else:
                ids_copy(slot).wait_recv()

    def take_block(slot):
        for c in range(PARTS):
            take(slot, c)
        take_ids(slot)

    def take_pair(slot):
        if (slot, PARTS + 1) not in taken:
            taken.add((slot, PARTS + 1))
            pair_copy(slot).wait_recv()

    def act(action):
        slot, c = action // (PARTS + 1), action % (PARTS + 1)
        if c == PARTS:
            for part_ in range(PARTS):
                take(slot, part_)
            pair_copy(slot).start()
            return
        parent = EDGES[slot - 1][0]
        take(parent, c)
        if c == PARTS - 1:
            take_ids(parent)
            ids_copy(slot).start()
        edge_copy(slot, c).start()

    def finish(slot):
        best = jnp.max(jnp.transpose(row_best[span(slot), :]), axis=0, keepdims=True)
        if slot > 0:
            best = jnp.maximum(best, col_best[slot])
        own_out[slot] = best
        if slot > 0:
            own_copy(slot).start()

    def span(slot):
        if isinstance(slot, int):
            return pl.ds(slot * ROWS, ROWS)
        return pl.ds(pl.multiple_of(slot * ROWS, ROWS), ROWS)

    def own_block():
        left = mine[0:ROWS, :]
        right = jnp.concatenate([left, other[0:ROWS, :]], axis=0)
        scores = lax.dot_general(
            left, right, (((1,), (1,)), ((), ())), preferred_element_type=jnp.float32)
        down = column_ids(ids[0, 0])
        down_ids[0:ROWS, :] = down
        same = lax.broadcasted_iota(jnp.int32, (ROWS, ROWS), 0) == lax.broadcasted_iota(
            jnp.int32, (ROWS, ROWS), 1)
        near = jnp.where((down == ids[0, 0]) & jnp.logical_not(same), scores[:, :ROWS], FLOOR)
        far = jnp.where(down == ids[0, 1], scores[:, ROWS:], FLOOR)
        row_best[0:ROWS, :] = jnp.maximum(near, far)

    def events(phase):
        if phase > 0:
            for group in PHASES[phase - 1][1:]:
                cross_copy(group[0]).start()
            for slot in range(SLOTS):
                if last_use(slot) == phase - 1:
                    finish(slot)
        if phase < len(PHASES):
            actions, *groups = PHASES[phase]
            for action in actions:
                act(action)
            for group in groups:
                take_block(group[0])
                take_pair(group[0])

    def lookup(phase, values):
        found = jnp.int32(values[0])
        for k, value in enumerate(values[1:], 1):
            found = jnp.where(phase == k, value, found)
        return found

    def packed(phase, member, first, count):
        code = lookup(phase, [
            sum(s << (5 * i) for i, s in enumerate(padded(groups[min(member, len(groups) - 1)])[first:first + count]))
            for _, *groups in PHASES])
        return [(code >> (5 * i)) & 31 for i in range(count)]

    def products(new, partners):
        left = jnp.concatenate([mine[span(p), :] for p in partners], axis=0)
        right = jnp.concatenate([mine[span(new), :], other[span(new), :]], axis=0)
        scores = lax.dot_general(
            left, right, (((1,), (1,)), ((), ())), preferred_element_type=jnp.float32)
        down_ids[span(new), :] = column_ids(ids[new, 0])
        top = [jnp.full((8, ROWS), FLOOR, jnp.float32)] * 2
        for i, p in enumerate(partners):
            down = down_ids[span(p), :]
            best = row_best[span(p), :]
            for half in range(2):
                block = scores[i * ROWS:(i + 1) * ROWS, half * ROWS:(half + 1) * ROWS]
                block = jnp.where(down == ids[new, half], block, FLOOR)
                best = jnp.maximum(best, block)
                top[half] = jnp.maximum(
                    top[half], jnp.max(block.reshape(ROWS // 8, 8, ROWS), axis=0))
            row_best[span(p), :] = best
        col_best[new] = jnp.max(top[0], axis=0, keepdims=True)
        cross_out[new] = jnp.max(top[1], axis=0, keepdims=True)

    def batch(phase):
        shape = lookup(phase, [SHAPES.index(shape_of(groups)) for _, *groups in PHASES])
        members = [packed(phase, m, 0, 5) + packed(phase, m, 5, 4) for m in range(2)]
        for index, (count, size) in enumerate(SHAPES):
            def run(count=count, size=size):
                for new, *partners in members[:count]:
                    products(new, partners[:size])
            pl.when(shape == index)(run)

    def dispatch(phase, low, high):
        if high - low == 1:
            events(low)
            return
        middle = (low + high) // 2
        pl.when(phase < middle)(lambda: dispatch(phase, low, middle))
        pl.when(phase >= middle)(lambda: dispatch(phase, middle, high))

    for c in range(PARTS):
        if c > 0:
            normalize_part(c)
        for action in FIRST:
            if action % (PARTS + 1) == c:
                act(action)
    act(PARTS)
    row_best[...] = jnp.full_like(row_best, FLOOR)
    take_pair(0)
    take_ids(0)
    own_block()

    def step(phase, carry):
        dispatch(phase, 0, len(PHASES))
        batch(phase)
        return carry

    lax.fori_loop(0, len(PHASES), step, 0)
    events(len(PHASES))

    def whole(ref, send, recv, first, count):
        rows = ref.at[pl.ds(first, count)]
        return pltpu.make_async_remote_copy(
            src_ref=rows, dst_ref=rows, send_sem=send.at[0], recv_sem=recv.at[0],
            device_id=sibling, device_id_type=MESH)

    whole(mine, part_send, part_send, 0, (SLOTS - 1) * ROWS).wait_send()
    whole(mine, pair_send, pair_send, 0, SLOTS * ROWS).wait_send()
    whole(ids, ids_send.at[pl.ds(1, 1)], ids_send.at[pl.ds(1, 1)], 0, SLOTS - 1).wait_send()
    own = whole(own_in, own_send, own_recv, 1, SLOTS - 1)
    cross = whole(cross_in, cross_send, cross_recv, 1, SLOTS - 1)
    own.wait_send()
    cross.wait_send()
    cross.wait_recv()
    own.wait_recv()
    best = own_out[0]
    for slot in range(1, SLOTS):
        best = jnp.maximum(best, jnp.maximum(own_in[slot], cross_in[slot]))
    out_ref[...] = best


def body(embeddings, cluster_ids, row_slots, cluster_sizes):
    dma = pltpu.SemaphoreType.DMA
    best = pl.pallas_call(
        kernel,
        out_shape=jax.ShapeDtypeStruct((1, ROWS), jnp.float32),
        in_specs=[pl.BlockSpec(memory_space=pl.ANY)] * 2,
        out_specs=pl.BlockSpec(memory_space=pltpu.VMEM),
        scratch_shapes=[
            pltpu.VMEM((ROWS, WIDTH), jnp.float32),
            pltpu.VMEM((SLOTS * ROWS, WIDTH), jnp.bfloat16),
            pltpu.VMEM((SLOTS * ROWS, WIDTH), jnp.bfloat16),
            pltpu.VMEM((SLOTS, 2, 1, ROWS), jnp.int32),
            pltpu.VMEM((SLOTS * ROWS, ROWS), jnp.int32),
            pltpu.VMEM((SLOTS * ROWS, ROWS), jnp.float32),
            pltpu.VMEM((SLOTS, 1, ROWS), jnp.float32),
            pltpu.VMEM((SLOTS, 1, ROWS), jnp.float32),
            pltpu.VMEM((SLOTS, 1, ROWS), jnp.float32),
            pltpu.VMEM((SLOTS, 1, ROWS), jnp.float32),
            pltpu.VMEM((SLOTS, 1, ROWS), jnp.float32),
            dma((1,)), dma((SLOTS, PARTS)), dma((2,)), dma((SLOTS,)),
            dma((1,)), dma((SLOTS,)), dma((1,)), dma((1,)),
            dma((1,)), dma((1,)), dma((PARTS + 1,)),
        ],
        compiler_params=pltpu.CompilerParams(
            collective_id=1, has_side_effects=True, vmem_limit_bytes=64 * 2**20 - 2**18),
    )(embeddings, cluster_ids.reshape(1, ROWS))
    return best.reshape(ROWS)


def solution(mesh):
    placed = (
        P(("grp", "blk"), None),
        P(("grp", "blk")),
        P(("grp", "blk")),
        P(("grp", "blk"), None),
    )
    return jax.shard_map(
        body, mesh=mesh, in_specs=placed, out_specs=P(("grp", "blk")), check_vma=False
    )
```

```python
import functools

import jax
import jax.numpy as jnp
from jax import lax
from jax.experimental import pallas as pl
from jax.experimental.pallas import tpu as pltpu
from jax.sharding import PartitionSpec as P

MESH = pl.DeviceIdType.MESH
ROWS = 128
WIDTH = 1024
NY, NZ, NX = 8, 8, 4
FLOOR = -4.0

STEPS = ((0, 0, 1), (0, 0, -1), (1, 0, 0), (-1, 0, 0), (0, 1, 0), (0, -1, 0))
EDGES = (
    (0, 3), (1, 3), (2, 3), (3, 0), (0, 1), (0, 2),
    (6, 2), (3, 3), (5, 5), (0, 4), (10, 4), (9, 5),
    (6, 0), (11, 4), (13, 0), (11, 1), (12, 5), (7, 2),
    (17, 1), (13, 2), (14, 4), (8, 0), (9, 1), (17, 5),
)
PARTS = 4
FIRST = (25, 30, 5, 50, 26, 31, 6, 51, 27, 32, 7, 52, 28, 33, 8, 53)
PHASES = (
    ((45, 65, 35, 10, 55, 46, 66, 36, 11, 56, 47, 67, 115, 60, 75, 37, 12, 57, 29, 34, 9, 54, 48, 68, 116, 38, 13, 58, 80, 61, 76), (1, 0)),
    ((117,), (5, 0)),
    ((90, 15, 70), (6, 1)),
    ((77, 81, 62), (10, 5, 1, 6)),
    ((91, 16, 71, 85, 49, 69, 78, 118, 92, 17, 72, 39, 14, 59, 63, 82, 93, 18, 73, 20, 86), (2, 6, 10)),
    ((83,), (9, 1, 2, 6, 10), (13, 0, 1, 5, 9, 10)),
    ((21, 95, 100, 40, 105, 87, 79, 119), (7, 9, 10)),
    ((), (11, 10, 0, 1, 2, 6, 7, 9)),
    ((22, 101, 41, 106, 88, 64), (23, 13, 1, 11, 7, 0, 2)),
    ((23, 102, 42, 107, 19, 74, 94, 96, 120, 84, 103, 43, 108, 110, 121, 97), (3, 5, 6, 13, 9, 10, 11), (12, 1, 2, 3, 6, 7, 11, 13, 23)),
    ((111, 98, 122, 89), (16, 6, 9, 13, 1, 0, 2), (18, 9, 10, 11, 12, 16, 23)),
    ((112, 24), (14, 1, 2, 3, 6, 7, 13, 18, 23)),
    ((123, 104, 113, 44, 109), (4, 7, 9, 10, 11, 12, 14, 16, 23), (17, 11, 1, 2, 3, 6, 7, 13, 18)),
    ((99,), (8, 9, 10, 11, 12, 14, 16, 17, 23), (20, 7, 11, 17, 10, 12, 14, 16, 23)),
    ((114, 124), (21, 0, 1, 2, 18, 4, 8, 13, 20), (19, 3, 13, 2, 4, 8, 14, 18, 20)),
    ((), (22, 2, 3, 23, 16, 14, 21), (24, 1, 2, 4, 18, 20, 22)),
    ((), (15, 2, 1, 3, 6, 14, 21)),
)
SLOTS = len(EDGES) + 1
PART = ROWS // PARTS


def tree_offsets():
    offsets = [(0, 0, 0)]
    for parent, way in EDGES:
        offsets.append(tuple(a + b for a, b in zip(offsets[parent], STEPS[way])))
    return offsets


OFFSETS = tree_offsets()
CHILDREN = [[s + 1 for s, edge in enumerate(EDGES) if edge[0] == p] for p in range(SLOTS)]
SINGLE, DOUBLE = (4, 6, 8), (6, 8)
WIDEST = 8


def last_use(slot):
    return max((k for k, (_, *groups) in enumerate(PHASES) if any(slot in g for g in groups)), default=0)


def hops(slot):
    return sum(min(a % n, n - a % n) for a, n in zip(OFFSETS[slot], (NY, NZ, NX)))


def shape_of(groups):
    sizes = SINGLE if len(groups) == 1 else DOUBLE
    return len(groups), min(s for s in sizes if s >= max(len(g) for g in groups) - 1)


SHAPES = sorted({shape_of(groups) for _, *groups in PHASES})


def padded(group):
    return group + group[-1:] * (WIDEST + 1 - len(group))


def normalize_rows(block):
    total = jnp.sum(block * block, axis=1, keepdims=True)
    return (block * lax.rsqrt(total + 1e-06)).astype(jnp.bfloat16)


def column_ids(row):
    return jnp.transpose(jnp.broadcast_to(row, (ROWS, ROWS)))


def kernel(
    rows_hbm, ids_hbm, out_ref,
    rows_ref, mine, other, ids, down_ids, row_best, col_best, own_out, own_in, cross_out, cross_in,
    part_send, part_recv, ids_send, ids_recv, pair_send, pair_recv,
    own_send, own_recv, cross_send, cross_recv, load_sem,
):
    grp = lax.axis_index("grp")
    blk = lax.axis_index("blk")
    y, core, z, x = grp // 2, grp % 2, blk // NX, blk % NX

    def at(offset, flip=False):
        ty = lax.rem(y + offset[0] % NY, NY)
        tz = lax.rem(z + offset[1] % NZ, NZ)
        tx = lax.rem(x + offset[2] % NX, NX)
        return (ty * 2 + (1 - core if flip else core), tz * NX + tx)

    def negated(offset):
        return tuple(-a for a in offset)

    sibling = at((0, 0, 0), True)
    behind = [at(negated(step)) for step in STEPS]

    def part(slot, c):
        return pl.ds(slot * ROWS + c * PART, PART)

    def edge_copy(slot, c):
        parent, way = EDGES[slot - 1]
        return pltpu.make_async_remote_copy(
            src_ref=mine.at[part(parent, c)], dst_ref=mine.at[part(slot, c)],
            send_sem=part_send.at[0], recv_sem=part_recv.at[slot, c],
            device_id=behind[way], device_id_type=MESH)

    def ids_copy(slot):
        if slot == 0:
            return pltpu.make_async_remote_copy(
                src_ref=ids.at[0, 0], dst_ref=ids.at[0, 1],
                send_sem=ids_send.at[0], recv_sem=ids_recv.at[0],
                device_id=sibling, device_id_type=MESH)
        parent, way = EDGES[slot - 1]
        return pltpu.make_async_remote_copy(
            src_ref=ids.at[parent], dst_ref=ids.at[slot],
            send_sem=ids_send.at[1], recv_sem=ids_recv.at[slot],
            device_id=behind[way], device_id_type=MESH)

    def pair_copy(slot):
        return pltpu.make_async_remote_copy(
            src_ref=mine.at[pl.ds(slot * ROWS, ROWS)], dst_ref=other.at[pl.ds(slot * ROWS, ROWS)],
            send_sem=pair_send.at[0], recv_sem=pair_recv.at[slot],
            device_id=sibling, device_id_type=MESH)

    def own_copy(slot):
        return pltpu.make_async_remote_copy(
            src_ref=own_out.at[slot], dst_ref=own_in.at[slot],
            send_sem=own_send.at[0], recv_sem=own_recv.at[0],
            device_id=at(OFFSETS[slot]), device_id_type=MESH)

    def cross_copy(slot):
        return pltpu.make_async_remote_copy(
            src_ref=cross_out.at[slot], dst_ref=cross_in.at[slot],
            send_sem=cross_send.at[0], recv_sem=cross_recv.at[0],
            device_id=at(OFFSETS[slot], True), device_id_type=MESH)

    barrier = pltpu.get_barrier_semaphore()
    peers = behind + [sibling]
    for peer in peers:
        pl.semaphore_signal(barrier, inc=1, device_id=peer, device_id_type=MESH)

    loads = [
        pltpu.make_async_copy(
            rows_hbm.at[pl.ds(c * PART, PART)], rows_ref.at[pl.ds(c * PART, PART)], load_sem.at[c])
        for c in range(PARTS)]
    loads.append(pltpu.make_async_copy(ids_hbm, ids.at[0, 0], load_sem.at[PARTS]))
    for load in loads:
        load.start()

    def normalize_part(c):
        loads[c].wait()
        mine[c * PART:(c + 1) * PART, :] = normalize_rows(rows_ref[c * PART:(c + 1) * PART, :])

    normalize_part(0)
    loads[PARTS].wait()
    pl.semaphore_wait(barrier, len(peers))
    ids_copy(0).start()
    taken = set()

    def take(slot, c):
        if slot > 0 and (slot, c) not in taken:
            taken.add((slot, c))
            edge_copy(slot, c).wait_recv()

    def take_ids(slot):
        if (slot, PARTS) not in taken:
            taken.add((slot, PARTS))
            if slot == 0:
                ids_copy(0).wait()
            else:
                ids_copy(slot).wait_recv()

    def take_block(slot):
        for c in range(PARTS):
            take(slot, c)
        take_ids(slot)

    def take_pair(slot):
        if (slot, PARTS + 1) not in taken:
            taken.add((slot, PARTS + 1))
            pair_copy(slot).wait_recv()

    def act(action):
        slot, c = action // (PARTS + 1), action % (PARTS + 1)
        if c == PARTS:
            for part_ in range(PARTS):
                take(slot, part_)
            pair_copy(slot).start()
            return
        parent = EDGES[slot - 1][0]
        take(parent, c)
        if c == PARTS - 1:
            take_ids(parent)
            ids_copy(slot).start()
        edge_copy(slot, c).start()

    def finish(slot):
        best = jnp.max(jnp.transpose(row_best[span(slot), :]), axis=0, keepdims=True)
        if slot > 0:
            best = jnp.maximum(best, col_best[slot])
        own_out[slot] = best
        if slot > 0:
            own_copy(slot).start()

    def span(slot):
        if isinstance(slot, int):
            return pl.ds(slot * ROWS, ROWS)
        return pl.ds(pl.multiple_of(slot * ROWS, ROWS), ROWS)

    def own_block():
        left = mine[0:ROWS, :]
        right = jnp.concatenate([left, other[0:ROWS, :]], axis=0)
        scores = lax.dot_general(
            left, right, (((1,), (1,)), ((), ())), preferred_element_type=jnp.float32)
        down = column_ids(ids[0, 0])
        down_ids[0:ROWS, :] = down
        same = lax.broadcasted_iota(jnp.int32, (ROWS, ROWS), 0) == lax.broadcasted_iota(
            jnp.int32, (ROWS, ROWS), 1)
        near = jnp.where((down == ids[0, 0]) & jnp.logical_not(same), scores[:, :ROWS], FLOOR)
        far = jnp.where(down == ids[0, 1], scores[:, ROWS:], FLOOR)
        row_best[0:ROWS, :] = jnp.maximum(near, far)

    def events(phase):
        if phase > 0:
            for group in PHASES[phase - 1][1:]:
                cross_copy(group[0]).start()
            for slot in sorted(range(SLOTS), key=hops, reverse=True):
                if last_use(slot) == phase - 1:
                    finish(slot)
        if phase < len(PHASES):
            actions, *groups = PHASES[phase]
            for action in actions:
                act(action)
            for group in groups:
                take_block(group[0])
                take_pair(group[0])

    def lookup(phase, values):
        found = jnp.int32(values[0])
        for k, value in enumerate(values[1:], 1):
            found = jnp.where(phase == k, value, found)
        return found

    def packed(phase, member, first, count):
        code = lookup(phase, [
            sum(s << (5 * i) for i, s in enumerate(padded(groups[min(member, len(groups) - 1)])[first:first + count]))
            for _, *groups in PHASES])
        return [(code >> (5 * i)) & 31 for i in range(count)]

    def products(new, partners):
        left = jnp.concatenate([mine[span(p), :] for p in partners], axis=0)
        right = jnp.concatenate([mine[span(new), :], other[span(new), :]], axis=0)
        scores = lax.dot_general(
            left, right, (((1,), (1,)), ((), ())), preferred_element_type=jnp.float32)
        down_ids[span(new), :] = column_ids(ids[new, 0])
        top = [jnp.full((8, ROWS), FLOOR, jnp.float32)] * 2
        for i, p in enumerate(partners):
            down = down_ids[span(p), :]
            best = row_best[span(p), :]
            for half in range(2):
                block = scores[i * ROWS:(i + 1) * ROWS, half * ROWS:(half + 1) * ROWS]
                block = jnp.where(down == ids[new, half], block, FLOOR)
                best = jnp.maximum(best, block)
                top[half] = jnp.maximum(
                    top[half], jnp.max(block.reshape(ROWS // 8, 8, ROWS), axis=0))
            row_best[span(p), :] = best
        col_best[new] = jnp.max(top[0], axis=0, keepdims=True)
        cross_out[new] = jnp.max(top[1], axis=0, keepdims=True)

    def batch(phase):
        shape = lookup(phase, [SHAPES.index(shape_of(groups)) for _, *groups in PHASES])
        members = [packed(phase, m, 0, 5) + packed(phase, m, 5, 4) for m in range(2)]
        for index, (count, size) in enumerate(SHAPES):
            def run(count=count, size=size):
                for new, *partners in members[:count]:
                    products(new, partners[:size])
            pl.when(shape == index)(run)

    def dispatch(phase, low, high):
        if high - low == 1:
            events(low)
            return
        middle = (low + high) // 2
        pl.when(phase < middle)(lambda: dispatch(phase, low, middle))
        pl.when(phase >= middle)(lambda: dispatch(phase, middle, high))

    for c in range(PARTS):
        if c > 0:
            normalize_part(c)
        for action in FIRST:
            if action % (PARTS + 1) == c:
                act(action)
    act(PARTS)
    row_best[...] = jnp.full_like(row_best, FLOOR)
    take_pair(0)
    take_ids(0)
    own_block()

    def step(phase, carry):
        dispatch(phase, 0, len(PHASES))
        batch(phase)
        return carry

    lax.fori_loop(0, len(PHASES), step, 0)
    events(len(PHASES))

    def whole(ref, send, recv, first, count):
        rows = ref.at[pl.ds(first, count)]
        return pltpu.make_async_remote_copy(
            src_ref=rows, dst_ref=rows, send_sem=send.at[0], recv_sem=recv.at[0],
            device_id=sibling, device_id_type=MESH)

    whole(mine, part_send, part_send, 0, (SLOTS - 1) * ROWS).wait_send()
    whole(mine, pair_send, pair_send, 0, SLOTS * ROWS).wait_send()
    whole(ids, ids_send.at[pl.ds(1, 1)], ids_send.at[pl.ds(1, 1)], 0, SLOTS - 1).wait_send()
    own = whole(own_in, own_send, own_recv, 1, SLOTS - 1)
    cross = whole(cross_in, cross_send, cross_recv, 1, SLOTS - 1)
    own.wait_send()
    cross.wait_send()
    cross.wait_recv()
    own.wait_recv()
    best = own_out[0]
    for slot in range(1, SLOTS):
        best = jnp.maximum(best, jnp.maximum(own_in[slot], cross_in[slot]))
    out_ref[...] = best[0]


def body(embeddings, cluster_ids, row_slots, cluster_sizes):
    dma = pltpu.SemaphoreType.DMA
    best = pl.pallas_call(
        kernel,
        out_shape=jax.ShapeDtypeStruct((ROWS,), jnp.float32),
        in_specs=[pl.BlockSpec(memory_space=pl.ANY)] * 2,
        out_specs=pl.BlockSpec(memory_space=pltpu.VMEM),
        scratch_shapes=[
            pltpu.VMEM((ROWS, WIDTH), jnp.float32),
            pltpu.VMEM((SLOTS * ROWS, WIDTH), jnp.bfloat16),
            pltpu.VMEM((SLOTS * ROWS, WIDTH), jnp.bfloat16),
            pltpu.VMEM((SLOTS, 2, 1, ROWS), jnp.int32),
            pltpu.VMEM((SLOTS * ROWS, ROWS), jnp.int32),
            pltpu.VMEM((SLOTS * ROWS, ROWS), jnp.float32),
            pltpu.VMEM((SLOTS, 1, ROWS), jnp.float32),
            pltpu.VMEM((SLOTS, 1, ROWS), jnp.float32),
            pltpu.VMEM((SLOTS, 1, ROWS), jnp.float32),
            pltpu.VMEM((SLOTS, 1, ROWS), jnp.float32),
            pltpu.VMEM((SLOTS, 1, ROWS), jnp.float32),
            dma((1,)), dma((SLOTS, PARTS)), dma((2,)), dma((SLOTS,)),
            dma((1,)), dma((SLOTS,)), dma((1,)), dma((1,)),
            dma((1,)), dma((1,)), dma((PARTS + 1,)),
        ],
        compiler_params=pltpu.CompilerParams(
            collective_id=1, has_side_effects=True, vmem_limit_bytes=64 * 2**20 - 2**18),
    )(embeddings, cluster_ids.reshape(1, ROWS))
    return best


def solution(mesh):
    placed = (
        P(("grp", "blk"), None),
        P(("grp", "blk")),
        P(("grp", "blk")),
        P(("grp", "blk"), None),
    )
    return jax.shard_map(
        body, mesh=mesh, in_specs=placed, out_specs=P(("grp", "blk")), check_vma=False
    )
```

```python
import functools

import jax
import jax.numpy as jnp
from jax import lax
from jax.experimental import pallas as pl
from jax.experimental.pallas import tpu as pltpu
from jax.sharding import PartitionSpec as P

MESH = pl.DeviceIdType.MESH
ROWS = 128
WIDTH = 1024
NY, NZ, NX = 8, 8, 4
FLOOR = -4.0

STEPS = ((0, 0, 1), (0, 0, -1), (1, 0, 0), (-1, 0, 0), (0, 1, 0), (0, -1, 0))
EDGES = (
    (0, 3), (1, 3), (2, 3), (3, 0), (0, 1), (0, 2),
    (6, 2), (3, 3), (5, 5), (0, 4), (10, 4), (9, 5),
    (6, 0), (11, 4), (13, 0), (11, 1), (12, 5), (7, 2),
    (17, 1), (13, 2), (14, 4), (8, 0), (9, 1), (17, 5),
)
PARTS = 2
FIRST = (15, 18, 3, 30, 16, 19, 4, 31)
PHASES = (
    ((27, 39, 21, 6, 33, 28, 17, 20, 40, 22, 7, 34, 5, 32, 69, 36, 45), (1, 0)),
    ((), (5, 1)),
    ((60,), (6, 0, 5)),
    ((48, 9, 42), (10, 5, 6)),
    ((37, 29, 46, 41, 61, 23, 10, 43, 8, 35, 49), (9, 1, 6)),
    ((), (13, 6, 5, 9, 10)),
    ((51,), (2, 5, 13, 9, 10)),
    ((), (7, 2, 9, 10)),
    ((12, 54, 24, 63), (11, 10, 0, 1, 2, 6, 7, 9, 13)),
    ((70, 52, 38, 47, 55, 62, 13, 25, 64, 11, 44, 50), (12, 0, 1, 2, 6, 7, 11, 13)),
    ((), (15, 2, 1, 6, 10, 11, 12)),
    ((57, 72), (3, 0, 9, 10, 11, 12, 15), (14, 0, 1, 2, 3, 6, 7, 12, 13)),
    ((66, 71), (20, 2, 0, 9, 10, 12, 14), (16, 3, 0, 2, 7, 12, 20)),
    ((58, 73, 53, 14), (23, 15, 13, 12, 11, 14, 0, 2, 20)),
    ((67, 26, 56, 65), (4, 0, 9, 10, 12, 14, 16, 23), (17, 1, 2, 3, 6, 7, 13, 15, 20)),
    ((), (8, 9, 10, 11, 12, 14, 16, 17, 23), (18, 9, 10, 11, 12, 14, 16, 17, 23)),
    ((59,), (21, 6, 7, 18, 4, 8, 13, 15, 20)),
    ((74, 68), (19, 1, 3, 2, 4, 8, 14, 18, 20)),
    ((), (22, 20, 23, 16, 19, 21), (24, 15, 2, 4, 18, 20, 22)),
)
SLOTS = len(EDGES) + 1
PART = ROWS // PARTS


def tree_offsets():
    offsets = [(0, 0, 0)]
    for parent, way in EDGES:
        offsets.append(tuple(a + b for a, b in zip(offsets[parent], STEPS[way])))
    return offsets


OFFSETS = tree_offsets()
CHILDREN = [[s + 1 for s, edge in enumerate(EDGES) if edge[0] == p] for p in range(SLOTS)]
SINGLE, DOUBLE = (4, 6, 8), (6, 8)
WIDEST = 8


def last_use(slot):
    return max((k for k, (_, *groups) in enumerate(PHASES) if any(slot in g for g in groups)), default=0)


def hops(slot):
    return sum(min(a % n, n - a % n) for a, n in zip(OFFSETS[slot], (NY, NZ, NX)))


def shape_of(groups):
    sizes = SINGLE if len(groups) == 1 else DOUBLE
    return len(groups), min(s for s in sizes if s >= max(len(g) for g in groups) - 1)


SHAPES = sorted({shape_of(groups) for _, *groups in PHASES})


def padded(group):
    return group + group[-1:] * (WIDEST + 1 - len(group))


def normalize_rows(block):
    total = jnp.sum(block * block, axis=1, keepdims=True)
    return (block * lax.rsqrt(total + 1e-06)).astype(jnp.bfloat16)


def column_ids(row):
    return jnp.transpose(jnp.broadcast_to(row, (ROWS, ROWS)))


def kernel(
    rows_hbm, ids_hbm, out_ref,
    rows_ref, mine, other, ids, down_ids, row_best, col_best, own_out, own_in, cross_out, cross_in,
    part_send, part_recv, ids_send, ids_recv, pair_send, pair_recv,
    own_send, own_recv, cross_send, cross_recv, load_sem,
):
    grp = lax.axis_index("grp")
    blk = lax.axis_index("blk")
    y, core, z, x = grp // 2, grp % 2, blk // NX, blk % NX

    def at(offset, flip=False):
        ty = lax.rem(y + offset[0] % NY, NY)
        tz = lax.rem(z + offset[1] % NZ, NZ)
        tx = lax.rem(x + offset[2] % NX, NX)
        return (ty * 2 + (1 - core if flip else core), tz * NX + tx)

    def negated(offset):
        return tuple(-a for a in offset)

    sibling = at((0, 0, 0), True)
    behind = [at(negated(step)) for step in STEPS]

    def part(slot, c):
        return pl.ds(slot * ROWS + c * PART, PART)

    def edge_copy(slot, c):
        parent, way = EDGES[slot - 1]
        return pltpu.make_async_remote_copy(
            src_ref=mine.at[part(parent, c)], dst_ref=mine.at[part(slot, c)],
            send_sem=part_send.at[0], recv_sem=part_recv.at[slot, c],
            device_id=behind[way], device_id_type=MESH)

    def ids_copy(slot):
        if slot == 0:
            return pltpu.make_async_remote_copy(
                src_ref=ids.at[0, 0], dst_ref=ids.at[0, 1],
                send_sem=ids_send.at[0], recv_sem=ids_recv.at[0],
                device_id=sibling, device_id_type=MESH)
        parent, way = EDGES[slot - 1]
        return pltpu.make_async_remote_copy(
            src_ref=ids.at[parent], dst_ref=ids.at[slot],
            send_sem=ids_send.at[1], recv_sem=ids_recv.at[slot],
            device_id=behind[way], device_id_type=MESH)

    def pair_copy(slot):
        return pltpu.make_async_remote_copy(
            src_ref=mine.at[pl.ds(slot * ROWS, ROWS)], dst_ref=other.at[pl.ds(slot * ROWS, ROWS)],
            send_sem=pair_send.at[0], recv_sem=pair_recv.at[slot],
            device_id=sibling, device_id_type=MESH)

    def own_copy(slot):
        return pltpu.make_async_remote_copy(
            src_ref=own_out.at[slot], dst_ref=own_in.at[slot],
            send_sem=own_send.at[0], recv_sem=own_recv.at[0],
            device_id=at(OFFSETS[slot]), device_id_type=MESH)

    def cross_copy(slot):
        return pltpu.make_async_remote_copy(
            src_ref=cross_out.at[slot], dst_ref=cross_in.at[slot],
            send_sem=cross_send.at[0], recv_sem=cross_recv.at[0],
            device_id=at(OFFSETS[slot], True), device_id_type=MESH)

    barrier = pltpu.get_barrier_semaphore()
    peers = behind + [sibling]
    for peer in peers:
        pl.semaphore_signal(barrier, inc=1, device_id=peer, device_id_type=MESH)

    loads = [
        pltpu.make_async_copy(
            rows_hbm.at[pl.ds(c * PART, PART)], rows_ref.at[pl.ds(c * PART, PART)], load_sem.at[c])
        for c in range(PARTS)]
    loads.append(pltpu.make_async_copy(ids_hbm, ids.at[0, 0], load_sem.at[PARTS]))
    for load in loads:
        load.start()

    def normalize_part(c):
        loads[c].wait()
        mine[c * PART:(c + 1) * PART, :] = normalize_rows(rows_ref[c * PART:(c + 1) * PART, :])

    normalize_part(0)
    loads[PARTS].wait()
    pl.semaphore_wait(barrier, len(peers))
    ids_copy(0).start()
    taken = set()

    def take(slot, c):
        if slot > 0 and (slot, c) not in taken:
            taken.add((slot, c))
            edge_copy(slot, c).wait_recv()

    def take_ids(slot):
        if (slot, PARTS) not in taken:
            taken.add((slot, PARTS))
            if slot == 0:
                ids_copy(0).wait()
            else:
                ids_copy(slot).wait_recv()

    def take_block(slot):
        for c in range(PARTS):
            take(slot, c)
        take_ids(slot)

    def take_pair(slot):
        if (slot, PARTS + 1) not in taken:
            taken.add((slot, PARTS + 1))
            pair_copy(slot).wait_recv()

    def act(action):
        slot, c = action // (PARTS + 1), action % (PARTS + 1)
        if c == PARTS:
            for part_ in range(PARTS):
                take(slot, part_)
            pair_copy(slot).start()
            return
        parent = EDGES[slot - 1][0]
        take(parent, c)
        if c == PARTS - 1:
            take_ids(parent)
            ids_copy(slot).start()
        edge_copy(slot, c).start()

    def finish(slot):
        best = jnp.max(jnp.transpose(row_best[span(slot), :]), axis=0, keepdims=True)
        if slot > 0:
            best = jnp.maximum(best, col_best[slot])
        own_out[slot] = best
        if slot > 0:
            own_copy(slot).start()

    def span(slot):
        if isinstance(slot, int):
            return pl.ds(slot * ROWS, ROWS)
        return pl.ds(pl.multiple_of(slot * ROWS, ROWS), ROWS)

    def own_block():
        left = mine[0:ROWS, :]
        right = jnp.concatenate([left, other[0:ROWS, :]], axis=0)
        scores = lax.dot_general(
            left, right, (((1,), (1,)), ((), ())), preferred_element_type=jnp.float32)
        down = column_ids(ids[0, 0])
        down_ids[0:ROWS, :] = down
        same = lax.broadcasted_iota(jnp.int32, (ROWS, ROWS), 0) == lax.broadcasted_iota(
            jnp.int32, (ROWS, ROWS), 1)
        near = jnp.where((down == ids[0, 0]) & jnp.logical_not(same), scores[:, :ROWS], FLOOR)
        far = jnp.where(down == ids[0, 1], scores[:, ROWS:], FLOOR)
        row_best[0:ROWS, :] = jnp.maximum(near, far)

    def events(phase):
        if phase > 0:
            for group in PHASES[phase - 1][1:]:
                cross_copy(group[0]).start()
            for slot in sorted(range(SLOTS), key=hops, reverse=True):
                if last_use(slot) == phase - 1:
                    finish(slot)
        if phase < len(PHASES):
            actions, *groups = PHASES[phase]
            for action in actions:
                act(action)
            for group in groups:
                take_block(group[0])
                take_pair(group[0])

    def lookup(phase, values):
        found = jnp.int32(values[0])
        for k, value in enumerate(values[1:], 1):
            found = jnp.where(phase == k, value, found)
        return found

    def packed(phase, member, first, count):
        code = lookup(phase, [
            sum(s << (5 * i) for i, s in enumerate(padded(groups[min(member, len(groups) - 1)])[first:first + count]))
            for _, *groups in PHASES])
        return [(code >> (5 * i)) & 31 for i in range(count)]

    def products(new, partners):
        left = jnp.concatenate([mine[span(p), :] for p in partners], axis=0)
        right = jnp.concatenate([mine[span(new), :], other[span(new), :]], axis=0)
        scores = lax.dot_general(
            left, right, (((1,), (1,)), ((), ())), preferred_element_type=jnp.float32)
        down_ids[span(new), :] = column_ids(ids[new, 0])
        top = [jnp.full((8, ROWS), FLOOR, jnp.float32)] * 2
        for i, p in enumerate(partners):
            down = down_ids[span(p), :]
            best = row_best[span(p), :]
            for half in range(2):
                block = scores[i * ROWS:(i + 1) * ROWS, half * ROWS:(half + 1) * ROWS]
                block = jnp.where(down == ids[new, half], block, FLOOR)
                best = jnp.maximum(best, block)
                top[half] = jnp.maximum(
                    top[half], jnp.max(block.reshape(ROWS // 8, 8, ROWS), axis=0))
            row_best[span(p), :] = best
        col_best[new] = jnp.max(top[0], axis=0, keepdims=True)
        cross_out[new] = jnp.max(top[1], axis=0, keepdims=True)

    def batch(phase):
        shape = lookup(phase, [SHAPES.index(shape_of(groups)) for _, *groups in PHASES])
        members = [packed(phase, m, 0, 5) + packed(phase, m, 5, 4) for m in range(2)]
        for index, (count, size) in enumerate(SHAPES):
            def run(count=count, size=size):
                for new, *partners in members[:count]:
                    products(new, partners[:size])
            pl.when(shape == index)(run)

    def dispatch(phase, low, high):
        if high - low == 1:
            events(low)
            return
        middle = (low + high) // 2
        pl.when(phase < middle)(lambda: dispatch(phase, low, middle))
        pl.when(phase >= middle)(lambda: dispatch(phase, middle, high))

    for c in range(PARTS):
        if c > 0:
            normalize_part(c)
        for action in FIRST:
            if action % (PARTS + 1) == c:
                act(action)
    act(PARTS)
    row_best[...] = jnp.full_like(row_best, FLOOR)
    take_pair(0)
    take_ids(0)
    own_block()

    def step(phase, carry):
        dispatch(phase, 0, len(PHASES))
        batch(phase)
        return carry

    lax.fori_loop(0, len(PHASES), step, 0)
    events(len(PHASES))

    def whole(ref, send, recv, first, count):
        rows = ref.at[pl.ds(first, count)]
        return pltpu.make_async_remote_copy(
            src_ref=rows, dst_ref=rows, send_sem=send.at[0], recv_sem=recv.at[0],
            device_id=sibling, device_id_type=MESH)

    whole(mine, part_send, part_send, 0, (SLOTS - 1) * ROWS).wait_send()
    whole(mine, pair_send, pair_send, 0, SLOTS * ROWS).wait_send()
    whole(ids, ids_send.at[pl.ds(1, 1)], ids_send.at[pl.ds(1, 1)], 0, SLOTS - 1).wait_send()
    own = whole(own_in, own_send, own_recv, 1, SLOTS - 1)
    cross = whole(cross_in, cross_send, cross_recv, 1, SLOTS - 1)
    own.wait_send()
    cross.wait_send()
    cross.wait_recv()
    own.wait_recv()
    best = own_out[0]
    for slot in range(1, SLOTS):
        best = jnp.maximum(best, jnp.maximum(own_in[slot], cross_in[slot]))
    out_ref[...] = best[0]


def body(embeddings, cluster_ids, row_slots, cluster_sizes):
    dma = pltpu.SemaphoreType.DMA
    best = pl.pallas_call(
        kernel,
        out_shape=jax.ShapeDtypeStruct((ROWS,), jnp.float32),
        in_specs=[pl.BlockSpec(memory_space=pl.ANY)] * 2,
        out_specs=pl.BlockSpec(memory_space=pltpu.VMEM),
        scratch_shapes=[
            pltpu.VMEM((ROWS, WIDTH), jnp.float32),
            pltpu.VMEM((SLOTS * ROWS, WIDTH), jnp.bfloat16),
            pltpu.VMEM((SLOTS * ROWS, WIDTH), jnp.bfloat16),
            pltpu.VMEM((SLOTS, 2, 1, ROWS), jnp.int32),
            pltpu.VMEM((SLOTS * ROWS, ROWS), jnp.int32),
            pltpu.VMEM((SLOTS * ROWS, ROWS), jnp.float32),
            pltpu.VMEM((SLOTS, 1, ROWS), jnp.float32),
            pltpu.VMEM((SLOTS, 1, ROWS), jnp.float32),
            pltpu.VMEM((SLOTS, 1, ROWS), jnp.float32),
            pltpu.VMEM((SLOTS, 1, ROWS), jnp.float32),
            pltpu.VMEM((SLOTS, 1, ROWS), jnp.float32),
            dma((1,)), dma((SLOTS, PARTS)), dma((2,)), dma((SLOTS,)),
            dma((1,)), dma((SLOTS,)), dma((1,)), dma((1,)),
            dma((1,)), dma((1,)), dma((PARTS + 1,)),
        ],
        compiler_params=pltpu.CompilerParams(
            collective_id=1, has_side_effects=True, vmem_limit_bytes=64 * 2**20 - 2**18),
    )(embeddings, cluster_ids.reshape(1, ROWS))
    return best


def solution(mesh):
    placed = (
        P(("grp", "blk"), None),
        P(("grp", "blk")),
        P(("grp", "blk")),
        P(("grp", "blk"), None),
    )
    return jax.shard_map(
        body, mesh=mesh, in_specs=placed, out_specs=P(("grp", "blk")), check_vma=False
    )
```
